768 devices in a mesh: rep: 96 (over y, z_lo, x), fsdp: 4 (over z_hi), tp: 2 (over core).
Axes of the slice: x: 4, y: 8, z: 12 (z_hi: 4, z_lo: 3; z = z_hi * 3 + z_lo), core: 2. Of those that a mesh axis runs over, the one named last changes fastest.
Arguments:
- grads: bfloat16 [96, 16384, 384], P('rep', 'fsdp', 'tp'), may hold values from -0.609375 to 0.609375
- slot_panels: int32 [768, 2], P('rep'), may hold values from -1 to 31, as said below
- factor_old: float32 [768, 512, 512], P(('rep', 'fsdp'), 'tp'), may hold values from -6 to 6
Outputs:
- factor_new: float32 [768, 512, 512], P(('rep', 'fsdp'), 'tp')
The draws below stay inside these ranges and needn't reach their ends.
Inputs may be any that keep to these rules, and one draw needn't show every extreme that they name: `slot_panels`: row r names the row panel i and the column panel j (i <= j) of the upper-triangle tile kept in slot r % 2 of owner r // 2, or -1 twice for an empty slot. Each of the 528 tiles stands in exactly one slot; every owner holds 1 tiles or one more, in its first slots.
All inputs are finite; a program needn't handle non-finite values.
Results may differ from the reference program's by a relative error of at most 0.0028.
Values may be sent and summed in bfloat16 or wider, within the bound.
No kernel may reach another device: no remote copies, remote signals or barrier semaphores. Data moves between devices by JAX's collectives and lax.ppermute only.
A program may use at most 64 MiB of HBM per device.

```python
import jax
import jax.numpy as jnp
import numpy as np
from jax import lax

M = 16384
TILE = 512
C = 384
PANELS = 32
TILES = 528
OWNERS = 384
SLOTS = 2
N_REP = 96


def draw_slot_panels(key, part):
    key = jax.random.fold_in(key, 11)
    row_table, col_table = np.triu_indices(PANELS)
    tile_key, owner_key = jax.random.split(key)
    tile_order = jax.random.permutation(tile_key, TILES)
    owner_order = jax.random.permutation(owner_key, OWNERS)
    turn = jnp.arange(TILES, dtype=jnp.int32)
    target = owner_order[turn % OWNERS] * SLOTS + turn // OWNERS
    row_ends = jnp.asarray(row_table, jnp.int32)[tile_order]
    col_ends = jnp.asarray(col_table, jnp.int32)[tile_order]
    pairs = jnp.stack([row_ends, col_ends], axis=1)
    table = jnp.full((OWNERS * SLOTS, 2), -1, jnp.int32)
    return table.at[target].set(pairs)


def shard_levels(key, dims, cuts, least, top_value):
    gain = 1.0
    for axis_at, parts in cuts:
        steps = jax.random.uniform(jax.random.fold_in(jax.random.fold_in(key, 6), axis_at), (parts,), jnp.float32, least / len(cuts), top_value / len(cuts))
        gain = gain * jnp.repeat(jnp.exp(steps), dims[axis_at] // parts).reshape((-1,) + (1,) * (len(dims) - 1 - axis_at))
    return gain


def gaussian(key, dims, scale, bound, shards=(), held_as=jnp.bfloat16):
    level = shard_levels(key, dims, shards, -0.22, 0.18) if shards else 1.0
    drawn = jax.random.normal(key, dims, jnp.float32) * scale * level
    return jnp.minimum(jnp.maximum(drawn, -bound), bound).astype(held_as)


def setup_inputs(seed: int = 0) -> dict:
    arg_keys = jax.random.split(jax.random.key(seed), 4)
    return {
        "grads": gaussian(arg_keys[0], (N_REP, M, C), (0.7 * N_REP ** -0.5), 0.609375, ((0, 96), (1, 4), (2, 2))),
        "slot_panels": draw_slot_panels(jax.random.fold_in(arg_keys[3], 71), 0),
        "factor_old": gaussian(arg_keys[2], (OWNERS * SLOTS, TILE, TILE), 1.0, 6.0, ((0, 384), (1, 2)), jnp.float32),
    }


def reference(grads, slot_panels, factor_old):
    def accumulate(total, replica):
        return total + replica.astype(jnp.float32), None

    total, _ = lax.scan(accumulate, jnp.zeros((M, C), jnp.float32), grads)
    summed = total.astype(jnp.bfloat16)
    panels = summed.reshape(M // TILE, TILE, C)

    def one_slot(inputs):
        ends, old_tile = inputs
        first_panel = panels[jnp.maximum(ends[0], 0)]
        second_panel = panels[jnp.maximum(ends[1], 0)]
        zero_tile = jnp.zeros((TILE, C), jnp.bfloat16)
        first_panel = jnp.where(ends[0] >= 0, first_panel, zero_tile)
        second_panel = jnp.where(ends[1] >= 0, second_panel, zero_tile)
        product = jnp.dot(first_panel, second_panel.T, preferred_element_type=jnp.float32)
        return 0.9 * old_tile + 0.1 * product

    return lax.map(one_slot, (slot_panels, factor_old))
```

```python
import jax
import jax.numpy as jnp
from jax import lax
from jax.experimental import pallas as pl
from jax.experimental.pallas import tpu as pltpu
from jax.sharding import Mesh
from jax.sharding import PartitionSpec as P

Y, ZL, X, F, T = 8, 3, 4, 4, 2
NEAR = ZL * X
REP = Y * NEAR
TILE = 512
HERE = 8
PANELS = HERE * F
PICKS = 4
LANES = 128
SUB = 8
QUARTERS = TILE // LANES


def pick_kernel(index_ref, table_ref, out_ref):
    def step(n, carry):
        for k in range(PICKS):
            out_ref[n, k] = table_ref[index_ref[n * PICKS + k]]
        return carry

    lax.fori_loop(0, REP, step, 0)


def pick_pieces(index, table):
    return pl.pallas_call(
        pick_kernel,
        out_shape=jax.ShapeDtypeStruct((REP, PICKS, SUB, LANES), table.dtype),
        in_specs=[
            pl.BlockSpec(memory_space=pltpu.SMEM),
            pl.BlockSpec(memory_space=pltpu.VMEM),
        ],
        out_specs=pl.BlockSpec(memory_space=pltpu.VMEM),
        compiler_params=pltpu.CompilerParams(vmem_limit_bytes=16 * 2**20),
        cost_estimate=pl.CostEstimate(flops=0, bytes_accessed=2 * 2**20, transcendentals=0),
    )(index, table)


def body(grads, slot_panels, factor_old):
    width = grads.shape[2]
    rows = grads.shape[1]
    place = lax.axis_index("fsdp")
    own = lax.dynamic_index_in_dim(slot_panels.reshape(F, PICKS), place, 0, keepdims=False)
    columns = grads[0].T.reshape(NEAR, width // NEAR, rows)
    note = jnp.pad(own.astype(grads.dtype), (0, LANES - PICKS))
    note = jnp.broadcast_to(note, (NEAR, width // NEAR, LANES))
    with jax.named_scope("exchange_near"):
        came = lax.all_to_all(
            jnp.concatenate([columns, note], axis=2), ("zl", "x"), 0, 0, tiled=True
        )
    near_sum = came[:, :, :rows].astype(jnp.float32).sum(0)
    near_ends = came[:, 0, rows : rows + PICKS].astype(jnp.float32)

    blocks = near_sum.reshape(2, SUB, HERE, QUARTERS, LANES).transpose(0, 3, 2, 1, 4)
    blocks = blocks.reshape(Y, HERE * SUB, LANES)
    note = jnp.pad(near_ends.reshape(-1), (0, SUB * LANES - NEAR * PICKS)).reshape(SUB, LANES)
    note = jnp.broadcast_to(note, (Y, SUB, LANES))
    with jax.named_scope("exchange_y"):
        came = lax.all_to_all(
            jnp.concatenate([blocks, note], axis=1), "y", 0, 0, tiled=True
        )
    summed = came[:, : HERE * SUB].sum(0).astype(jnp.bfloat16)
    ends = came[:, HERE * SUB, : NEAR * PICKS].reshape(REP * PICKS).astype(jnp.int32)

    with jax.named_scope("gather_fsdp"):
        table = lax.all_to_all(
            jnp.broadcast_to(summed, (F, HERE * SUB, LANES)), "fsdp", 0, 0, tiled=True
        )
    table = table.reshape(PANELS, SUB, LANES)
    with jax.named_scope("pick"):
        pieces = pick_pieces(jnp.maximum(ends, 0), table)
    with jax.named_scope("exchange_panels"):
        came = lax.all_to_all(
            pieces.reshape(REP, PICKS * SUB, LANES), ("y", "zl", "x"), 0, 0, tiled=True
        )
    came = came.reshape(2, QUARTERS, NEAR, 2, 2, SUB, LANES)
    panels = came.transpose(3, 4, 2, 0, 5, 1, 6).reshape(2, 2, width, TILE)
    first = panels[:, 0].reshape(2, width, T, TILE // T).transpose(2, 0, 1, 3)
    second = jnp.broadcast_to(panels[:, 1], (T, 2, width, TILE))
    with jax.named_scope("exchange_tp"):
        both = lax.all_to_all(
            jnp.concatenate([first, second], axis=3), "tp", 0, 0, tiled=True
        )
    first = both[..., : TILE // T]
    second = both[..., TILE // T :]
    product = jnp.einsum("tsca,tscb->sab", first, second, preferred_element_type=jnp.float32)
    valid = own[0::2] >= 0
    product = jnp.where(valid[:, None, None], product, 0.0)
    return 0.9 * factor_old + 0.1 * product


def solution(mesh):
    fine = Mesh(mesh.devices.reshape(Y, ZL, X, F, T), ("y", "zl", "x", "fsdp", "tp"))
    rep = ("y", "zl", "x")
    placed = (P(rep, "fsdp", "tp"), P(rep, None), P(rep + ("fsdp",), "tp", None))
    return jax.shard_map(
        body, mesh=fine, in_specs=placed, out_specs=P(rep + ("fsdp",), "tp", None), check_vma=False
    )
```

```python
import jax
import jax.numpy as jnp
from jax import lax
from jax.experimental import pallas as pl
from jax.experimental.pallas import tpu as pltpu
from jax.sharding import Mesh
from jax.sharding import PartitionSpec as P

YH, YL, ZL, X, F, T = 4, 2, 3, 4, 4, 2
NEAR = YL * ZL * X
PLANE = YH * YL * X
TILE = 512
HERE = 8
PANELS = HERE * F
PICKS = 4
LANES = 128
SUB = 8


def pick_kernel(index_ref, table_ref, out_ref):
    def step(n, carry):
        for k in range(PICKS):
            panel = index_ref[n * PICKS + k]
            for z in range(ZL):
                out_ref[n, k, z] = table_ref[z * PANELS + panel]
        return carry

    lax.fori_loop(0, PLANE, step, 0, unroll=4)


def pick_pieces(index, table):
    return pl.pallas_call(
        pick_kernel,
        out_shape=jax.ShapeDtypeStruct((PLANE, PICKS, ZL, SUB, LANES), table.dtype),
        in_specs=[
            pl.BlockSpec(memory_space=pltpu.SMEM),
            pl.BlockSpec(memory_space=pltpu.VMEM),
        ],
        out_specs=pl.BlockSpec(memory_space=pltpu.VMEM),
        compiler_params=pltpu.CompilerParams(vmem_limit_bytes=16 * 2**20),
        cost_estimate=pl.CostEstimate(flops=0, bytes_accessed=2 * 2**20, transcendentals=0),
    )(index, table)


def body(grads, slot_panels, factor_old):
    width = grads.shape[2]
    rows = grads.shape[1]
    place = lax.axis_index("fsdp")
    turn = jnp.arange(F * 2, dtype=jnp.int32)[:, None]
    own = [jnp.where(turn == 2 * place + s, slot_panels, 0).sum(0) for s in range(2)]
    own = jnp.concatenate(own)
    columns = grads[0].T.reshape(NEAR, SUB, rows)
    note = jnp.pad(own.astype(grads.dtype), (0, LANES - PICKS))
    note = jnp.broadcast_to(note, (NEAR, SUB, LANES))
    with jax.named_scope("exchange_near"):
        came = lax.all_to_all(
            jnp.concatenate([columns, note], axis=2), ("yl", "zl", "x"), 0, 0, tiled=True
        )
    near_sum = came[:, :, :rows].astype(jnp.float32).sum(0)
    near_ends = came[:, 0, rows : rows + PICKS].astype(jnp.float32)

    blocks = near_sum.reshape(SUB, HERE, YH, LANES).transpose(2, 1, 0, 3)
    blocks = blocks.reshape(YH, HERE * SUB, LANES)
    note = jnp.pad(near_ends.reshape(-1), (0, LANES - NEAR * PICKS))
    note = jnp.broadcast_to(note, (YH, SUB, LANES))
    with jax.named_scope("exchange_far"):
        came = lax.all_to_all(
            jnp.concatenate([blocks, note], axis=1), "yh", 0, 0, tiled=True
        )
    summed = came[:, : HERE * SUB].sum(0).astype(jnp.bfloat16)
    ends = came[:, HERE * SUB, : NEAR * PICKS].astype(jnp.int32)
    ends = ends.reshape(YH, YL, ZL, X * PICKS)
    ends = lax.dynamic_index_in_dim(ends, lax.axis_index("zl"), 2, keepdims=False)
    ends = jnp.maximum(ends, 0).reshape(PLANE * PICKS)

    with jax.named_scope("gather_z"):
        table = lax.all_to_all(
            jnp.broadcast_to(summed, (ZL * F, HERE * SUB, LANES)), ("zl", "fsdp"), 0, 0, tiled=True
        )
    table = table.reshape(ZL * PANELS, SUB, LANES)
    with jax.named_scope("pick"):
        pieces = pick_pieces(ends, table)
    with jax.named_scope("exchange_panels"):
        came = lax.all_to_all(
            pieces.reshape(PLANE, PICKS * ZL * SUB, LANES), ("yh", "yl", "x"), 0, 0, tiled=True
        )
    came = came.reshape(YH, YL, X, 2, 2, ZL, SUB, LANES)
    panels = came.transpose(3, 4, 1, 5, 2, 6, 0, 7).reshape(2, 2, width, TILE)
    first = panels[:, 0].reshape(2, width, T, TILE // T).transpose(2, 0, 1, 3)
    second = jnp.broadcast_to(panels[:, 1], (T, 2, width, TILE))
    with jax.named_scope("exchange_tp"):
        both = lax.all_to_all(
            jnp.concatenate([first, second], axis=3), "tp", 0, 0, tiled=True
        )
    first = both[..., : TILE // T]
    second = both[..., TILE // T :]
    product = jnp.einsum("tsca,tscb->sab", first, second, preferred_element_type=jnp.float32)
    valid = own[0::2] >= 0
    product = jnp.where(valid[:, None, None], product, 0.0)
    return 0.9 * factor_old + 0.1 * product


def solution(mesh):
    fine = Mesh(
        mesh.devices.reshape(YH, YL, ZL, X, F, T), ("yh", "yl", "zl", "x", "fsdp", "tp")
    )
    rep = ("yh", "yl", "zl", "x")
    placed = (P(rep, "fsdp", "tp"), P(rep, None), P(rep + ("fsdp",), "tp", None))
    return jax.shard_map(
        body, mesh=fine, in_specs=placed, out_specs=P(rep + ("fsdp",), "tp", None), check_vma=False
    )
```

```python
import jax
import jax.numpy as jnp
from jax import lax
from jax.experimental import pallas as pl
from jax.experimental.pallas import tpu as pltpu
from jax.sharding import Mesh
from jax.sharding import PartitionSpec as P

YH, YL, ZL, X, F, T = 4, 2, 3, 4, 4, 2
NEAR = YL * ZL * X
PLANE = YH * YL * X
TILE = 512
HERE = 8
PANELS = HERE * F
PICKS = 4
LANES = 128
SUB = 8
CHUNKS = 6


def note_kernel(ends_ref, columns_ref, out_ref, note_ref, sems):
    width, rows = columns_ref.shape
    step = width // CHUNKS
    copies = []
    for n in range(CHUNKS):
        part = pl.ds(n * step, step)
        copies.append(
            pltpu.make_async_copy(
                columns_ref.at[part], out_ref.at[part, pl.ds(0, rows)], sems.at[n]
            )
        )
        copies[-1].start()
    place = lax.axis_index("fsdp")
    lane = lax.broadcasted_iota(jnp.int32, note_ref.shape, 1)
    note = jnp.zeros(note_ref.shape, jnp.int32)
    for slot in range(2):
        for end in range(2):
            note = jnp.where(lane == 2 * slot + end, ends_ref[end, 2 * place + slot], note)
    note_ref[...] = note.astype(jnp.float32).astype(note_ref.dtype)
    copies.append(
        pltpu.make_async_copy(note_ref, out_ref.at[:, pl.ds(rows, LANES)], sems.at[CHUNKS])
    )
    copies[-1].start()
    for copy in copies:
        copy.wait()


def add_note(slot_panels, columns):
    width, rows = columns.shape
    return pl.pallas_call(
        note_kernel,
        out_shape=jax.ShapeDtypeStruct((width, rows + LANES), columns.dtype),
        in_specs=[
            pl.BlockSpec(memory_space=pltpu.SMEM),
            pl.BlockSpec(memory_space=pl.ANY),
        ],
        out_specs=pl.BlockSpec(memory_space=pl.ANY),
        scratch_shapes=[
            pltpu.VMEM((width, LANES), columns.dtype),
            pltpu.SemaphoreType.DMA((CHUNKS + 1,)),
        ],
        compiler_params=pltpu.CompilerParams(vmem_limit_bytes=16 * 2**20),
        cost_estimate=pl.CostEstimate(flops=0, bytes_accessed=3 * 2**20, transcendentals=0),
    )(slot_panels.T, columns)


def pick_kernel(index_ref, table_ref, out_ref):
    def step(n, carry):
        panels = [index_ref[n * PICKS + k] for k in range(PICKS)]
        found = [[table_ref[z * PANELS + panel] for z in range(ZL)] for panel in panels]
        for k in range(PICKS):
            for z in range(ZL):
                out_ref[n, k, z] = found[k][z]
        return carry

    lax.fori_loop(0, PLANE, step, 0, unroll=4)


def pick_pieces(index, table):
    return pl.pallas_call(
        pick_kernel,
        out_shape=jax.ShapeDtypeStruct((PLANE, PICKS, ZL, SUB, LANES), table.dtype),
        in_specs=[
            pl.BlockSpec(memory_space=pltpu.SMEM),
            pl.BlockSpec(memory_space=pltpu.VMEM),
        ],
        out_specs=pl.BlockSpec(memory_space=pltpu.VMEM),
        compiler_params=pltpu.CompilerParams(vmem_limit_bytes=16 * 2**20),
        cost_estimate=pl.CostEstimate(flops=0, bytes_accessed=2 * 2**20, transcendentals=0),
    )(index, table)


def body(grads, slot_panels, factor_old):
    width = grads.shape[2]
    rows = grads.shape[1]
    place = lax.axis_index("fsdp")
    turn = jnp.arange(F * 2, dtype=jnp.int32)[:, None]
    own = [jnp.where(turn == 2 * place + s, slot_panels, 0).sum(0) for s in range(2)]
    own = jnp.concatenate(own)
    with jax.named_scope("add_note"):
        noted = add_note(slot_panels, grads[0].T)
    with jax.named_scope("exchange_near"):
        came = lax.all_to_all(
            noted.reshape(NEAR, SUB, rows + LANES), ("yl", "zl", "x"), 0, 0, tiled=True
        )
    near_sum = came[:, :, :rows].astype(jnp.float32).sum(0)
    near_ends = came[:, 0, rows : rows + PICKS].astype(jnp.float32)

    blocks = near_sum.reshape(SUB, HERE, YH, LANES).transpose(2, 1, 0, 3)
    blocks = blocks.reshape(YH, HERE * SUB, LANES)
    note = jnp.pad(near_ends.reshape(-1), (0, LANES - NEAR * PICKS))
    note = jnp.broadcast_to(note, (YH, SUB, LANES))
    with jax.named_scope("exchange_far"):
        came = lax.all_to_all(
            jnp.concatenate([blocks, note], axis=1), "yh", 0, 0, tiled=True
        )
    summed = came[:, : HERE * SUB].sum(0).astype(jnp.bfloat16)
    ends = came[:, HERE * SUB, : NEAR * PICKS].astype(jnp.int32)
    ends = ends.reshape(YH, YL, ZL, X * PICKS)
    ends = lax.dynamic_index_in_dim(ends, lax.axis_index("zl"), 2, keepdims=False)
    ends = jnp.maximum(ends, 0).reshape(PLANE * PICKS)

    with jax.named_scope("gather_z"):
        table = lax.all_to_all(
            jnp.broadcast_to(summed, (ZL * F, HERE * SUB, LANES)), ("zl", "fsdp"), 0, 0, tiled=True
        )
    table = table.reshape(ZL * PANELS, SUB, LANES)
    with jax.named_scope("pick"):
        pieces = pick_pieces(ends, table)
    with jax.named_scope("exchange_panels"):
        came = lax.all_to_all(
            pieces.reshape(PLANE, PICKS * ZL * SUB, LANES), ("yh", "yl", "x"), 0, 0, tiled=True
        )
    came = came.reshape(T, YH // T, YL, X, 2, 2, ZL, SUB, LANES)
    second = came[..., 1, :, :, :].transpose(4, 2, 5, 3, 6, 0, 1, 7).reshape(2, width, TILE)
    half = lax.axis_index("tp")

    def row_half(place):
        part = lax.dynamic_index_in_dim(came[..., 0, :, :, :], place, 0, keepdims=False)
        return part.transpose(3, 1, 4, 2, 5, 0, 6).reshape(2, width, TILE // T)

    with jax.named_scope("exchange_tp"):
        other = lax.ppermute(
            jnp.concatenate([row_half(1 - half), second], axis=2), "tp", [(0, 1), (1, 0)]
        )
    product = jnp.einsum(
        "sca,scb->sab", row_half(half), second, preferred_element_type=jnp.float32
    )
    product = product + jnp.einsum(
        "sca,scb->sab",
        other[..., : TILE // T],
        other[..., TILE // T :],
        preferred_element_type=jnp.float32,
    )
    valid = own[0::2] >= 0
    product = jnp.where(valid[:, None, None], product, 0.0)
    return 0.9 * factor_old + 0.1 * product


def solution(mesh):
    fine = Mesh(
        mesh.devices.reshape(YH, YL, ZL, X, F, T), ("yh", "yl", "zl", "x", "fsdp", "tp")
    )
    rep = ("yh", "yl", "zl", "x")
    placed = (P(rep, "fsdp", "tp"), P(rep, None), P(rep + ("fsdp",), "tp", None))
    return jax.shard_map(
        body, mesh=fine, in_specs=placed, out_specs=P(rep + ("fsdp",), "tp", None), check_vma=False
    )
```

```python
import jax
import jax.numpy as jnp
from jax import lax
from jax.experimental import pallas as pl
from jax.experimental.pallas import tpu as pltpu
from jax.sharding import Mesh
from jax.sharding import PartitionSpec as P

YH, YL, ZL, X, F, T = 4, 2, 3, 4, 4, 2
NEAR = YL * ZL * X
PLANE = YH * YL * X
TILE = 512
HERE = 8
PANELS = HERE * F
PICKS = 4
LANES = 128
SUB = 8
CHUNKS = 6


def note_kernel(panels_ref, columns_ref, out_ref, ends_ref, note_ref, sems):
    width, rows = columns_ref.shape
    step = width // CHUNKS
    copies = []
    for n in range(CHUNKS):
        part = pl.ds(n * step, step)
        copies.append(
            pltpu.make_async_copy(
                columns_ref.at[part], out_ref.at[part, pl.ds(0, rows)], sems.at[n]
            )
        )
        copies[-1].start()
    ends = pltpu.make_async_copy(panels_ref, ends_ref, sems.at[CHUNKS + 1])
    ends.start()
    ends.wait()
    place = lax.axis_index("fsdp")
    lane = lax.broadcasted_iota(jnp.int32, note_ref.shape, 1)
    note = jnp.zeros(note_ref.shape, jnp.int32)
    for slot in range(2):
        for end in range(2):
            note = jnp.where(lane == 2 * slot + end, ends_ref[end, 2 * place + slot], note)
    note_ref[...] = note.astype(jnp.float32).astype(note_ref.dtype)
    copies.append(
        pltpu.make_async_copy(note_ref, out_ref.at[:, pl.ds(rows, LANES)], sems.at[CHUNKS])
    )
    copies[-1].start()
    for copy in copies:
        copy.wait()


def add_note(slot_panels, columns):
    width, rows = columns.shape
    return pl.pallas_call(
        note_kernel,
        out_shape=jax.ShapeDtypeStruct((width, rows + LANES), columns.dtype),
        in_specs=[pl.BlockSpec(memory_space=pltpu.HBM)] * 2,
        out_specs=pl.BlockSpec(memory_space=pl.ANY),
        scratch_shapes=[
            pltpu.SMEM(slot_panels.shape[::-1], slot_panels.dtype),
            pltpu.VMEM((width, LANES), columns.dtype),
            pltpu.SemaphoreType.DMA((CHUNKS + 2,)),
        ],
        cost_estimate=pl.CostEstimate(flops=0, bytes_accessed=3 * 2**20, transcendentals=0),
    )(slot_panels.T, columns)


def pick_kernel(index_ref, table_ref, out_ref):
    def step(n, carry):
        panels = [index_ref[n * PICKS + k] for k in range(PICKS)]
        found = [[table_ref[z * PANELS + panel] for z in range(ZL)] for panel in panels]
        for k in range(PICKS):
            for z in range(ZL):
                out_ref[n, k, z] = found[k][z]
        return carry

    lax.fori_loop(0, PLANE, step, 0, unroll=4)


def pick_pieces(index, table):
    return pl.pallas_call(
        pick_kernel,
        out_shape=jax.ShapeDtypeStruct((PLANE, PICKS, ZL, SUB, LANES), table.dtype),
        in_specs=[
            pl.BlockSpec(memory_space=pltpu.SMEM),
            pl.BlockSpec(memory_space=pltpu.VMEM),
        ],
        out_specs=pl.BlockSpec(memory_space=pltpu.VMEM),
        compiler_params=pltpu.CompilerParams(vmem_limit_bytes=16 * 2**20),
        cost_estimate=pl.CostEstimate(flops=0, bytes_accessed=2 * 2**20, transcendentals=0),
    )(index, table)


def body(grads, slot_panels, factor_old):
    width = grads.shape[2]
    rows = grads.shape[1]
    place = lax.axis_index("fsdp")
    turn = jnp.arange(F * 2, dtype=jnp.int32)[:, None]
    own = [jnp.where(turn == 2 * place + s, slot_panels, 0).sum(0) for s in range(2)]
    own = jnp.concatenate(own)
    with jax.named_scope("add_note"):
        noted = add_note(slot_panels, grads[0].T)
    with jax.named_scope("exchange_near"):
        came = lax.all_to_all(
            noted.reshape(NEAR, SUB, rows + LANES), ("yl", "zl", "x"), 0, 0, tiled=True
        )
    near_sum = came[:, :, :rows].astype(jnp.float32).sum(0)
    near_ends = came[:, 0, rows : rows + PICKS].astype(jnp.float32)

    blocks = near_sum.reshape(SUB, HERE, YH, LANES).transpose(2, 1, 0, 3)
    blocks = blocks.reshape(YH, HERE * SUB, LANES)
    note = jnp.pad(near_ends.reshape(-1), (0, LANES - NEAR * PICKS))
    note = jnp.broadcast_to(note, (YH, SUB, LANES))
    with jax.named_scope("exchange_far"):
        came = lax.all_to_all(
            jnp.concatenate([blocks, note], axis=1), "yh", 0, 0, tiled=True
        )
    summed = came[:, : HERE * SUB].sum(0).astype(jnp.bfloat16)
    ends = came[:, HERE * SUB, : NEAR * PICKS].astype(jnp.int32)
    ends = ends.reshape(YH, YL, ZL, X * PICKS)
    ends = lax.dynamic_index_in_dim(ends, lax.axis_index("zl"), 2, keepdims=False)
    ends = jnp.maximum(ends, 0).reshape(PLANE * PICKS)

    with jax.named_scope("gather_z"):
        table = lax.all_to_all(
            jnp.broadcast_to(summed, (ZL * F, HERE * SUB, LANES)), ("zl", "fsdp"), 0, 0, tiled=True
        )
    table = table.reshape(ZL * PANELS, SUB, LANES)
    with jax.named_scope("pick"):
        pieces = pick_pieces(ends, table)
    with jax.named_scope("exchange_panels"):
        came = lax.all_to_all(
            pieces.reshape(PLANE, PICKS * ZL * SUB, LANES), ("yh", "yl", "x"), 0, 0, tiled=True
        )
    came = came.reshape(T, YH // T, YL, X, 2, 2, ZL, SUB, LANES)
    second = came[..., 1, :, :, :].transpose(4, 2, 5, 3, 6, 0, 1, 7).reshape(2, width, TILE)
    half = lax.axis_index("tp")

    def row_half(place):
        part = lax.dynamic_index_in_dim(came[..., 0, :, :, :], place, 0, keepdims=False)
        return part.transpose(3, 1, 4, 2, 5, 0, 6).reshape(2, width, TILE // T)

    with jax.named_scope("exchange_tp"):
        other = lax.ppermute(
            jnp.concatenate([row_half(1 - half), second], axis=2), "tp", [(0, 1), (1, 0)]
        )
    product = jnp.einsum(
        "sca,scb->sab", row_half(half), second, preferred_element_type=jnp.float32
    )
    product = product + jnp.einsum(
        "sca,scb->sab",
        other[..., : TILE // T],
        other[..., TILE // T :],
        preferred_element_type=jnp.float32,
    )
    valid = own[0::2] >= 0
    product = jnp.where(valid[:, None, None], product, 0.0)
    return 0.9 * factor_old + 0.1 * product


def solution(mesh):
    fine = Mesh(
        mesh.devices.reshape(YH, YL, ZL, X, F, T), ("yh", "yl", "zl", "x", "fsdp", "tp")
    )
    rep = ("yh", "yl", "zl", "x")
    placed = (P(rep, "fsdp", "tp"), P(rep, None), P(rep + ("fsdp",), "tp", None))
    return jax.shard_map(
        body, mesh=fine, in_specs=placed, out_specs=P(rep + ("fsdp",), "tp", None), check_vma=False
    )
```

```python
import jax
import jax.numpy as jnp
from jax import lax
from jax.experimental import pallas as pl
from jax.experimental.pallas import tpu as pltpu
from jax.sharding import Mesh
from jax.sharding import PartitionSpec as P

YH, YL, ZL, X, F, T = 4, 2, 3, 4, 4, 2
NEAR = YL * X
FAR = YH * ZL
PLANE = YH * NEAR
TILE = 512
HERE = 8
PANELS = HERE * F
PICKS = 4
LANES = 128
SUB = 8


def pick_kernel(index_ref, table_ref, out_ref):
    def step(n, carry):
        panels = [index_ref[n * PICKS + k] for k in range(PICKS)]
        found = [[table_ref[z * PANELS + panel] for z in range(ZL)] for panel in panels]
        for k in range(PICKS):
            for z in range(ZL):
                out_ref[n, k, z] = found[k][z]
        return carry

    lax.fori_loop(0, PLANE, step, 0, unroll=4)


def pick_pieces(index, table):
    return pl.pallas_call(
        pick_kernel,
        out_shape=jax.ShapeDtypeStruct((PLANE, PICKS, ZL, SUB, LANES), table.dtype),
        in_specs=[
            pl.BlockSpec(memory_space=pltpu.SMEM),
            pl.BlockSpec(memory_space=pltpu.VMEM),
        ],
        out_specs=pl.BlockSpec(memory_space=pltpu.VMEM),
        compiler_params=pltpu.CompilerParams(vmem_limit_bytes=16 * 2**20),
        cost_estimate=pl.CostEstimate(flops=0, bytes_accessed=2 * 2**20, transcendentals=0),
    )(index, table)


def body(grads, slot_panels, factor_old):
    width = grads.shape[2]
    rows = grads.shape[1]
    place = lax.axis_index("fsdp")
    turn = jnp.arange(F * 2, dtype=jnp.int32)[:, None]
    own = [jnp.where(turn == 2 * place + s, slot_panels, 0).sum(0) for s in range(2)]
    own = jnp.concatenate(own)
    columns = grads[0].T.reshape(NEAR, width // NEAR, rows)
    note = jnp.pad(own.astype(grads.dtype), (0, LANES - PICKS))
    note = jnp.broadcast_to(note, (NEAR, width // NEAR, LANES))
    with jax.named_scope("exchange_near"):
        came = lax.all_to_all(
            jnp.concatenate([columns, note], axis=2), ("yl", "x"), 0, 0, tiled=True
        )
    near_sum = came[:, :, :rows].astype(jnp.float32).sum(0)
    near_ends = came[:, 0, rows : rows + PICKS].astype(jnp.float32)

    blocks = near_sum.reshape(ZL, SUB, HERE, YH, LANES).transpose(3, 0, 2, 1, 4)
    blocks = blocks.reshape(FAR, HERE * SUB, LANES)
    note = jnp.pad(near_ends.reshape(-1), (0, LANES - NEAR * PICKS))
    note = jnp.broadcast_to(note, (FAR, SUB, LANES))
    with jax.named_scope("exchange_far"):
        came = lax.all_to_all(
            jnp.concatenate([blocks, note], axis=1), ("yh", "zl"), 0, 0, tiled=True
        )
    summed = came[:, : HERE * SUB].sum(0).astype(jnp.bfloat16)
    ends = came[:, HERE * SUB, : NEAR * PICKS].astype(jnp.int32)
    ends = ends.reshape(YH, ZL, NEAR * PICKS)
    ends = lax.dynamic_index_in_dim(ends, lax.axis_index("zl"), 1, keepdims=False)
    ends = jnp.maximum(ends, 0).reshape(PLANE * PICKS)

    with jax.named_scope("gather_z"):
        table = lax.all_to_all(
            jnp.broadcast_to(summed, (ZL * F, HERE * SUB, LANES)), ("zl", "fsdp"), 0, 0, tiled=True
        )
    table = table.reshape(ZL * PANELS, SUB, LANES)
    with jax.named_scope("pick"):
        pieces = pick_pieces(ends, table)
    with jax.named_scope("exchange_panels"):
        came = lax.all_to_all(
            pieces.reshape(PLANE, PICKS * ZL * SUB, LANES), ("yh", "yl", "x"), 0, 0, tiled=True
        )
    came = came.reshape(T, YH // T, YL, X, 2, 2, ZL, SUB, LANES)
    second = came[..., 1, :, :, :].transpose(4, 2, 3, 5, 6, 0, 1, 7).reshape(2, width, TILE)
    half = lax.axis_index("tp")

    def row_half(place):
        part = lax.dynamic_index_in_dim(came[..., 0, :, :, :], place, 0, keepdims=False)
        return part.transpose(3, 1, 2, 4, 5, 0, 6).reshape(2, width, TILE // T)

    with jax.named_scope("exchange_tp"):
        other = lax.ppermute(
            jnp.concatenate([row_half(1 - half), second], axis=2), "tp", [(0, 1), (1, 0)]
        )
    product = jnp.einsum(
        "sca,scb->sab", row_half(half), second, preferred_element_type=jnp.float32
    )
    product = product + jnp.einsum(
        "sca,scb->sab",
        other[..., : TILE // T],
        other[..., TILE // T :],
        preferred_element_type=jnp.float32,
    )
    valid = own[0::2] >= 0
    product = jnp.where(valid[:, None, None], product, 0.0)
    return 0.9 * factor_old + 0.1 * product


def solution(mesh):
    fine = Mesh(
        mesh.devices.reshape(YH, YL, ZL, X, F, T), ("yh", "yl", "zl", "x", "fsdp", "tp")
    )
    rep = ("yh", "yl", "zl", "x")
    placed = (P(rep, "fsdp", "tp"), P(rep, None), P(rep + ("fsdp",), "tp", None))
    return jax.shard_map(
        body, mesh=fine, in_specs=placed, out_specs=P(rep + ("fsdp",), "tp", None), check_vma=False
    )
```

```python
import jax
import jax.numpy as jnp
from jax import lax
from jax.experimental import pallas as pl
from jax.experimental.pallas import tpu as pltpu
from jax.sharding import Mesh
from jax.sharding import PartitionSpec as P

YH, YL, ZL, X, F, T = 4, 2, 3, 4, 4, 2
NEAR = YL * ZL * X
PLANE = YH * YL * X
TILE = 512
HERE = 8
PANELS = HERE * F
PICKS = 4
LANES = 128
SUB = 8
PART = 8


def pick_kernel(index_ref, table_ref, out_ref):
    first = pl.program_id(0) * PART

    def step(n, carry):
        panels = [index_ref[(first + n) * PICKS + k] for k in range(PICKS)]
        found = [[table_ref[z * PANELS + panel] for z in range(ZL)] for panel in panels]
        for k in range(PICKS):
            for z in range(ZL):
                out_ref[n, k, z] = found[k][z]
        return carry

    lax.fori_loop(0, PART, step, 0, unroll=4)


def pick_pieces(index, table):
    return pl.pallas_call(
        pick_kernel,
        out_shape=jax.ShapeDtypeStruct((PLANE, PICKS, ZL, SUB, LANES), table.dtype),
        grid=(PLANE // PART,),
        in_specs=[
            pl.BlockSpec(memory_space=pltpu.SMEM),
            pl.BlockSpec(memory_space=pltpu.VMEM),
        ],
        out_specs=pl.BlockSpec((PART, PICKS, ZL, SUB, LANES), lambda n: (n, 0, 0, 0, 0)),
        compiler_params=pltpu.CompilerParams(vmem_limit_bytes=16 * 2**20),
        cost_estimate=pl.CostEstimate(flops=0, bytes_accessed=2 * 2**20, transcendentals=0),
    )(index, table)


def body(grads, slot_panels, factor_old):
    width = grads.shape[2]
    rows = grads.shape[1]
    place = lax.axis_index("fsdp")
    turn = jnp.arange(F * 2, dtype=jnp.int32)[:, None]
    own = [jnp.where(turn == 2 * place + s, slot_panels, 0).sum(0) for s in range(2)]
    own = jnp.concatenate(own)
    columns = grads[0].T.reshape(NEAR, width // NEAR, rows)
    note = jnp.pad(own.astype(grads.dtype), (0, LANES - PICKS))
    note = jnp.broadcast_to(note, (NEAR, width // NEAR, LANES))
    with jax.named_scope("exchange_near"):
        came = lax.all_to_all(
            jnp.concatenate([columns, note], axis=2), ("yl", "zl", "x"), 0, 0, tiled=True
        )
    near_sum = came[:, :, :rows].astype(jnp.float32).sum(0)
    near_ends = came[:, 0, rows : rows + PICKS].astype(jnp.float32)

    blocks = near_sum.reshape(SUB, HERE, YH, LANES).transpose(2, 1, 0, 3)
    blocks = blocks.reshape(YH, HERE * SUB, LANES)
    note = jnp.pad(near_ends.reshape(-1), (0, LANES - NEAR * PICKS))
    note = jnp.broadcast_to(note, (YH, SUB, LANES))
    with jax.named_scope("exchange_far"):
        came = lax.all_to_all(
            jnp.concatenate([blocks, note], axis=1), "yh", 0, 0, tiled=True
        )
    summed = came[:, : HERE * SUB].sum(0).astype(jnp.bfloat16)
    ends = came[:, HERE * SUB, : NEAR * PICKS].astype(jnp.int32)
    ends = ends.reshape(YH, YL, ZL, X * PICKS)
    ends = lax.dynamic_index_in_dim(ends, lax.axis_index("zl"), 2, keepdims=False)
    ends = jnp.maximum(ends, 0).reshape(PLANE * PICKS)

    with jax.named_scope("gather_z"):
        table = lax.all_to_all(
            jnp.broadcast_to(summed, (ZL * F, HERE * SUB, LANES)), ("zl", "fsdp"), 0, 0, tiled=True
        )
    table = table.reshape(ZL * PANELS, SUB, LANES)
    with jax.named_scope("pick"):
        pieces = pick_pieces(ends, table)
    with jax.named_scope("exchange_panels"):
        came = lax.all_to_all(
            pieces.reshape(PLANE, PICKS * ZL * SUB, LANES), ("yh", "yl", "x"), 0, 0, tiled=True
        )
    came = came.reshape(T, YH // T, YL, X, 2, 2, ZL, SUB, LANES)
    second = came[..., 1, :, :, :].transpose(4, 2, 5, 3, 6, 0, 1, 7).reshape(2, width, TILE)
    half = lax.axis_index("tp")

    def row_half(place):
        part = lax.dynamic_index_in_dim(came[..., 0, :, :, :], place, 0, keepdims=False)
        return part.transpose(3, 1, 4, 2, 5, 0, 6).reshape(2, width, TILE // T)

    with jax.named_scope("exchange_tp"):
        other = lax.ppermute(
            jnp.concatenate([row_half(1 - half), second], axis=2), "tp", [(0, 1), (1, 0)]
        )
    product = jnp.einsum(
        "sca,scb->sab", row_half(half), second, preferred_element_type=jnp.float32
    )
    product = product + jnp.einsum(
        "sca,scb->sab",
        other[..., : TILE // T],
        other[..., TILE // T :],
        preferred_element_type=jnp.float32,
    )
    valid = own[0::2] >= 0
    product = jnp.where(valid[:, None, None], product, 0.0)
    return 0.9 * factor_old + 0.1 * product


def solution(mesh):
    fine = Mesh(
        mesh.devices.reshape(YH, YL, ZL, X, F, T), ("yh", "yl", "zl", "x", "fsdp", "tp")
    )
    rep = ("yh", "yl", "zl", "x")
    placed = (P(rep, "fsdp", "tp"), P(rep, None), P(rep + ("fsdp",), "tp", None))
    return jax.shard_map(
        body, mesh=fine, in_specs=placed, out_specs=P(rep + ("fsdp",), "tp", None), check_vma=False
    )
```

```python
import jax
import jax.numpy as jnp
from jax import lax
from jax.experimental import pallas as pl
from jax.experimental.pallas import tpu as pltpu
from jax.sharding import Mesh
from jax.sharding import PartitionSpec as P

YH, YL, ZL, X, F, T = 4, 2, 3, 4, 4, 2
NEAR = YL * ZL * X
PLANE = YH * YL * X
TILE = 512
HERE = 8
PANELS = HERE * F
PICKS = 4
LANES = 128
SUB = 8


def pick_kernel(index_ref, table_ref, out_ref):
    def step(n, carry):
        panels = [index_ref[n * PICKS + k] for k in range(PICKS)]
        found = [[table_ref[z * PANELS + panel] for z in range(ZL)] for panel in panels]
        for k in range(PICKS):
            for z in range(ZL):
                out_ref[n, k, z] = found[k][z]
        return carry

    lax.fori_loop(0, PLANE, step, 0, unroll=4)


def pick_pieces(index, table):
    return pl.pallas_call(
        pick_kernel,
        out_shape=jax.ShapeDtypeStruct((PLANE, PICKS, ZL, SUB, LANES), table.dtype),
        in_specs=[
            pl.BlockSpec(memory_space=pltpu.SMEM),
            pl.BlockSpec(memory_space=pltpu.VMEM),
        ],
        out_specs=pl.BlockSpec(memory_space=pltpu.VMEM),
        compiler_params=pltpu.CompilerParams(vmem_limit_bytes=16 * 2**20),
        cost_estimate=pl.CostEstimate(flops=0, bytes_accessed=2 * 2**20, transcendentals=0),
    )(index, table)


def body(grads, slot_panels, factor_old):
    width = grads.shape[2]
    rows = grads.shape[1]
    place = lax.axis_index("fsdp")
    turn = jnp.arange(F * 2, dtype=jnp.int32)[:, None]
    own = [jnp.where(turn == 2 * place + s, slot_panels, 0).sum(0) for s in range(2)]
    own = jnp.concatenate(own)
    columns = grads[0].T.reshape(NEAR, width // NEAR, rows)
    note = jnp.pad(own.astype(grads.dtype), (0, LANES - PICKS))
    note = jnp.broadcast_to(note, (NEAR, width // NEAR, LANES))
    with jax.named_scope("exchange_near"):
        came = lax.all_to_all(
            jnp.concatenate([columns, note], axis=2), ("yl", "zl", "x"), 0, 0, tiled=True
        )
    near_sum = came[:, :, :rows].astype(jnp.float32).sum(0)
    near_ends = came[:, 0, rows : rows + PICKS].astype(jnp.float32)

    blocks = near_sum.reshape(SUB, HERE, YH, LANES).transpose(2, 1, 0, 3)
    blocks = blocks.reshape(YH, HERE * SUB, LANES)
    note = jnp.pad(near_ends.reshape(-1), (0, LANES - NEAR * PICKS))
    note = jnp.broadcast_to(note, (YH, SUB, LANES))
    with jax.named_scope("exchange_far"):
        came = lax.all_to_all(
            jnp.concatenate([blocks, note], axis=1), "yh", 0, 0, tiled=True
        )
    summed = came[:, : HERE * SUB].sum(0).astype(jnp.bfloat16)
    ends = came[:, HERE * SUB, : NEAR * PICKS].astype(jnp.int32)
    ends = ends.reshape(YH, YL, ZL, X * PICKS)
    ends = lax.dynamic_index_in_dim(ends, lax.axis_index("zl"), 2, keepdims=False)
    ends = jnp.maximum(ends, 0).reshape(PLANE * PICKS)

    with jax.named_scope("gather_z"):
        table = lax.all_to_all(
            jnp.broadcast_to(summed, (ZL * F, HERE * SUB, LANES)), ("zl", "fsdp"), 0, 0, tiled=True
        )
    table = table.reshape(ZL * PANELS, SUB, LANES)
    with jax.named_scope("pick"):
        pieces = pick_pieces(ends, table)
    with jax.named_scope("exchange_panels"):
        came = lax.all_to_all(
            pieces.reshape(PLANE, PICKS * ZL * SUB, LANES), ("yh", "yl", "x"), 0, 0, tiled=True
        )
    came = came.reshape(T, YH // T, YL, X, 2, 2, ZL, SUB, LANES)
    second = came[..., 1, :, :, :].transpose(4, 2, 5, 3, 6, 0, 1, 7).reshape(2, width, TILE)
    half = lax.axis_index("tp")

    def row_half(place):
        part = lax.dynamic_index_in_dim(came[..., 0, :, :, :], place, 0, keepdims=False)
        return part.transpose(3, 1, 4, 2, 5, 0, 6).reshape(2, width, TILE // T)

    with jax.named_scope("exchange_tp"):
        other = lax.ppermute(
            jnp.concatenate([row_half(1 - half), second], axis=2), "tp", [(0, 1), (1, 0)]
        )
    product = jnp.einsum(
        "sca,scb->sab", row_half(half), second, preferred_element_type=jnp.float32
    )
    product = product + jnp.einsum(
        "sca,scb->sab",
        other[..., : TILE // T],
        other[..., TILE // T :],
        preferred_element_type=jnp.float32,
    )
    valid = own[0::2] >= 0
    product = jnp.where(valid[:, None, None], product, 0.0)
    return 0.9 * factor_old + 0.1 * product


def solution(mesh):
    fine = Mesh(
        mesh.devices.reshape(YH, YL, ZL, X, F, T), ("yh", "yl", "zl", "x", "fsdp", "tp")
    )
    rep = ("yh", "yl", "zl", "x")
    placed = (P(rep, "fsdp", "tp"), P(rep, None), P(rep + ("fsdp",), "tp", None))
    return jax.shard_map(
        body, mesh=fine, in_specs=placed, out_specs=P(rep + ("fsdp",), "tp", None), check_vma=False
    )
```

```python
import jax
import jax.numpy as jnp
from jax import lax
from jax.experimental import pallas as pl
from jax.experimental.pallas import tpu as pltpu
from jax.sharding import Mesh
from jax.sharding import PartitionSpec as P

YH, YL, ZL, X, F, T = 4, 2, 3, 4, 4, 2
NEAR = YL * ZL * X
PLANE = YH * YL * X
TILE = 512
HERE = 8
PANELS = HERE * F
PICKS = 4
LANES = 128
SUB = 8


def pick_kernel(index_ref, table_ref, out_ref):
    def step(n, carry):
        found = [table_ref[index_ref[n * PICKS + k]] for k in range(PICKS)]
        for k in range(PICKS):
            out_ref[n * PICKS + k] = found[k]
        return carry

    lax.fori_loop(0, PLANE, step, 0, unroll=8)


def pick_pieces(index, table):
    return pl.pallas_call(
        pick_kernel,
        out_shape=jax.ShapeDtypeStruct((PLANE * PICKS, ZL * SUB, LANES), table.dtype),
        in_specs=[
            pl.BlockSpec(memory_space=pltpu.SMEM),
            pl.BlockSpec(memory_space=pltpu.VMEM),
        ],
        out_specs=pl.BlockSpec(memory_space=pltpu.VMEM),
        compiler_params=pltpu.CompilerParams(vmem_limit_bytes=16 * 2**20),
        cost_estimate=pl.CostEstimate(flops=0, bytes_accessed=2 * 2**20, transcendentals=0),
    )(index, table)


def body(grads, slot_panels, factor_old):
    width = grads.shape[2]
    rows = grads.shape[1]
    place = lax.axis_index("fsdp")
    turn = jnp.arange(F * 2, dtype=jnp.int32)[:, None]
    own = [jnp.where(turn == 2 * place + s, slot_panels, 0).sum(0) for s in range(2)]
    own = jnp.concatenate(own)
    columns = grads[0].T.reshape(NEAR, width // NEAR, rows)
    note = jnp.pad(own.astype(grads.dtype), (0, LANES - PICKS))
    note = jnp.broadcast_to(note, (NEAR, width // NEAR, LANES))
    with jax.named_scope("exchange_near"):
        came = lax.all_to_all(
            jnp.concatenate([columns, note], axis=2), ("yl", "zl", "x"), 0, 0, tiled=True
        )
    near_sum = came[:, :, :rows].astype(jnp.float32).sum(0)
    near_ends = came[:, 0, rows : rows + PICKS].astype(jnp.float32)

    blocks = near_sum.reshape(SUB, HERE, YH, LANES).transpose(2, 1, 0, 3)
    blocks = blocks.reshape(YH, HERE * SUB, LANES)
    note = jnp.pad(near_ends.reshape(-1), (0, LANES - NEAR * PICKS))
    note = jnp.broadcast_to(note, (YH, SUB, LANES))
    with jax.named_scope("exchange_far"):
        came = lax.all_to_all(
            jnp.concatenate([blocks, note], axis=1), "yh", 0, 0, tiled=True
        )
    summed = came[:, : HERE * SUB].sum(0).astype(jnp.bfloat16)
    ends = came[:, HERE * SUB, : NEAR * PICKS].astype(jnp.int32)
    ends = ends.reshape(YH, YL, ZL, X * PICKS)
    ends = lax.dynamic_index_in_dim(ends, lax.axis_index("zl"), 2, keepdims=False)
    ends = jnp.maximum(ends, 0).reshape(PLANE * PICKS)

    with jax.named_scope("gather_z"):
        table = lax.all_to_all(
            jnp.broadcast_to(summed, (ZL * F, HERE * SUB, LANES)), ("zl", "fsdp"), 0, 0, tiled=True
        )
    table = table.reshape(ZL, PANELS, SUB, LANES).transpose(1, 0, 2, 3)
    table = table.reshape(PANELS, ZL * SUB, LANES)
    with jax.named_scope("pick"):
        pieces = pick_pieces(ends, table)
    with jax.named_scope("exchange_panels"):
        came = lax.all_to_all(
            pieces.reshape(PLANE, PICKS * ZL * SUB, LANES), ("yh", "yl", "x"), 0, 0, tiled=True
        )
    came = came.reshape(T, YH // T, YL, X, 2, 2, ZL, SUB, LANES)
    second = came[..., 1, :, :, :].transpose(4, 2, 5, 3, 6, 0, 1, 7).reshape(2, width, TILE)
    half = lax.axis_index("tp")

    def row_half(place):
        part = lax.dynamic_index_in_dim(came[..., 0, :, :, :], place, 0, keepdims=False)
        return part.transpose(3, 1, 4, 2, 5, 0, 6).reshape(2, width, TILE // T)

    with jax.named_scope("exchange_tp"):
        other = lax.ppermute(
            jnp.concatenate([row_half(1 - half), second], axis=2), "tp", [(0, 1), (1, 0)]
        )
    product = jnp.einsum(
        "sca,scb->sab", row_half(half), second, preferred_element_type=jnp.float32
    )
    product = product + jnp.einsum(
        "sca,scb->sab",
        other[..., : TILE // T],
        other[..., TILE // T :],
        preferred_element_type=jnp.float32,
    )
    valid = own[0::2] >= 0
    product = jnp.where(valid[:, None, None], product, 0.0)
    return 0.9 * factor_old + 0.1 * product


def solution(mesh):
    fine = Mesh(
        mesh.devices.reshape(YH, YL, ZL, X, F, T), ("yh", "yl", "zl", "x", "fsdp", "tp")
    )
    rep = ("yh", "yl", "zl", "x")
    placed = (P(rep, "fsdp", "tp"), P(rep, None), P(rep + ("fsdp",), "tp", None))
    return jax.shard_map(
        body, mesh=fine, in_specs=placed, out_specs=P(rep + ("fsdp",), "tp", None), check_vma=False
    )
```

```python
import jax
import jax.numpy as jnp
from jax import lax
from jax.experimental import pallas as pl
from jax.experimental.pallas import tpu as pltpu
from jax.sharding import Mesh
from jax.sharding import PartitionSpec as P

YH, YL, ZL, X, F, T = 4, 2, 3, 4, 4, 2
NEAR = YL * ZL * X
PLANE = YH * YL * X
TILE = 512
HERE = 8
PANELS = HERE * F
PICKS = 4
LANES = 128
SUB = 8


def pick_kernel(index_ref, table_ref, out_ref):
    def step(n, carry):
        panels = [index_ref[n * PICKS + k] for k in range(PICKS)]
        found = [[table_ref[z * PANELS + panel] for z in range(ZL)] for panel in panels]
        for k in range(PICKS):
            for z in range(ZL):
                out_ref[n, k, z] = found[k][z]
        return carry

    lax.fori_loop(0, PLANE, step, 0, unroll=4)


def pick_pieces(index, table):
    return pl.pallas_call(
        pick_kernel,
        out_shape=jax.ShapeDtypeStruct((PLANE, PICKS, ZL, SUB, LANES), table.dtype),
        in_specs=[
            pl.BlockSpec(memory_space=pltpu.SMEM),
            pl.BlockSpec(memory_space=pltpu.VMEM),
        ],
        out_specs=pl.BlockSpec(memory_space=pltpu.VMEM),
        compiler_params=pltpu.CompilerParams(vmem_limit_bytes=16 * 2**20),
        cost_estimate=pl.CostEstimate(flops=0, bytes_accessed=2 * 2**20, transcendentals=0),
    )(index, table)


def body(grads, slot_panels, factor_old):
    width = grads.shape[2]
    rows = grads.shape[1]
    place = lax.axis_index("fsdp")
    turn = jnp.arange(F * 2, dtype=jnp.int32)[:, None]
    own = [jnp.where(turn == 2 * place + s, slot_panels, 0).sum(0) for s in range(2)]
    own = jnp.concatenate(own)
    columns = grads[0].T.reshape(NEAR, width // NEAR, rows)
    note = slot_panels.T.astype(grads.dtype)
    note = jnp.pad(note, ((0, SUB - 2), (0, LANES - F * 2)))
    note = jnp.broadcast_to(note, (NEAR, SUB, LANES))
    with jax.named_scope("exchange_near"):
        came = lax.all_to_all(
            jnp.concatenate([columns, note], axis=2), ("yl", "zl", "x"), 0, 0, tiled=True
        )
    near_sum = came[:, :, :rows].astype(jnp.float32).sum(0)
    near_ends = came[:, :2, rows : rows + F * 2].astype(jnp.float32)
    near_ends = lax.dynamic_slice_in_dim(near_ends, 2 * place, 2, axis=2).transpose(0, 2, 1)

    blocks = near_sum.reshape(SUB, HERE, YH, LANES).transpose(2, 1, 0, 3)
    blocks = blocks.reshape(YH, HERE * SUB, LANES)
    note = jnp.pad(near_ends.reshape(-1), (0, LANES - NEAR * PICKS))
    note = jnp.broadcast_to(note, (YH, SUB, LANES))
    with jax.named_scope("exchange_far"):
        came = lax.all_to_all(
            jnp.concatenate([blocks, note], axis=1), "yh", 0, 0, tiled=True
        )
    summed = came[:, : HERE * SUB].sum(0).astype(jnp.bfloat16)
    ends = came[:, HERE * SUB, : NEAR * PICKS].astype(jnp.int32)
    ends = ends.reshape(YH, YL, ZL, X * PICKS)
    ends = lax.dynamic_index_in_dim(ends, lax.axis_index("zl"), 2, keepdims=False)
    ends = jnp.maximum(ends, 0).reshape(PLANE * PICKS)

    with jax.named_scope("gather_z"):
        table = lax.all_to_all(
            jnp.broadcast_to(summed, (ZL * F, HERE * SUB, LANES)), ("zl", "fsdp"), 0, 0, tiled=True
        )
    table = table.reshape(ZL * PANELS, SUB, LANES)
    with jax.named_scope("pick"):
        pieces = pick_pieces(ends, table)
    with jax.named_scope("exchange_panels"):
        came = lax.all_to_all(
            pieces.reshape(PLANE, PICKS * ZL * SUB, LANES), ("yh", "yl", "x"), 0, 0, tiled=True
        )
    came = came.reshape(T, YH // T, YL, X, 2, 2, ZL, SUB, LANES)
    second = came[..., 1, :, :, :].transpose(4, 2, 5, 3, 6, 0, 1, 7).reshape(2, width, TILE)
    half = lax.axis_index("tp")

    def row_half(place):
        part = lax.dynamic_index_in_dim(came[..., 0, :, :, :], place, 0, keepdims=False)
        return part.transpose(3, 1, 4, 2, 5, 0, 6).reshape(2, width, TILE // T)

    with jax.named_scope("exchange_tp"):
        other = lax.ppermute(
            jnp.concatenate([row_half(1 - half), second], axis=2), "tp", [(0, 1), (1, 0)]
        )
    product = jnp.einsum(
        "sca,scb->sab", row_half(half), second, preferred_element_type=jnp.float32
    )
    product = product + jnp.einsum(
        "sca,scb->sab",
        other[..., : TILE // T],
        other[..., TILE // T :],
        preferred_element_type=jnp.float32,
    )
    valid = own[0::2] >= 0
    product = jnp.where(valid[:, None, None], product, 0.0)
    return 0.9 * factor_old + 0.1 * product


def solution(mesh):
    fine = Mesh(
        mesh.devices.reshape(YH, YL, ZL, X, F, T), ("yh", "yl", "zl", "x", "fsdp", "tp")
    )
    rep = ("yh", "yl", "zl", "x")
    placed = (P(rep, "fsdp", "tp"), P(rep, None), P(rep + ("fsdp",), "tp", None))
    return jax.shard_map(
        body, mesh=fine, in_specs=placed, out_specs=P(rep + ("fsdp",), "tp", None), check_vma=False
    )
```
